32 devices in a mesh: mode: 4 (over x, core), member: 8 (over z, y).
Axes of the slice: x: 2, y: 2, z: 4, core: 2. Of those that a mesh axis runs over, the one named last changes fastest.
Arguments:
- ground_accel: bfloat16 [4, 639], replicated, may hold values from -6 to 6
- modal_kernel: bfloat16 [4096, 512], P(('mode', 'member')), may hold values from -0.25 to 0.25
- mode_shapes: bfloat16 [49152, 4096], P('member', 'mode'), may hold values from -0.09375 to 0.09375
- member_owner: int32 [8192, 1], P('member'), may hold values from 0 to 31; in each aligned block of 256 rows (0 to 255, 256 to 511, ...) at most 16 rows name the same one
- member_group: int32 [8192, 1], P('member'), may hold values from 0 to 3
- record_table: int32 [128, 8], P(('mode', 'member')), may hold values from 0 to 3
- case_coef: float32 [8, 6], replicated, may hold values from -1.5 to 1.5
- gravity: float32 [128, 8], P(('mode', 'member')), may hold values from -10 to 10
Outputs:
- demand: float32 [128, 8], P(('mode', 'member'))
The draws below stay inside these ranges and needn't reach their ends.
Inputs may be any that keep to these rules, and one draw needn't show every extreme that they name: `member_owner`: in each aligned block of 1024 / 4 members no owner is named more than 16 times, a bound that some block reaches.
All inputs are finite; a program needn't handle non-finite values.
Results may differ from the reference program's by a relative error of at most 0.0065.
Values may be sent and summed in bfloat16 or wider, within the bound.
A program may use at most 64 MiB of HBM per device.

```python
import math
import jax
import jax.numpy as jnp
import numpy as np
from jax import lax

MODES = 4096
TAPS = 512
COMPS = 6
RECORDS = 4
CASES = 8
TW = 128
MEM_DEV = 1024
GROUP_DEV = 4
CAP = 16
SPAN = 639
MEMBERS = 8192
GROUPS = 128
N_MODE = 4
N_MEMBER = 8


def plant(array, stream_key, low, high):
    longest = array.shape.index(max(array.shape))
    spots = []
    for shift in (0, 1):
        where = [jax.random.randint(jax.random.fold_in(stream_key, axis), (), 0, length) for axis, length in enumerate(array.shape)]
        where[longest] = (where[longest] + shift) % array.shape[longest]
        spots.append(tuple(where))
    return array.at[spots[0]].set(low).at[spots[1]].set(high)


def block_levels(key, shape, shards, low, largest):
    gain = 1.0
    for position, shards_of in shards:
        steps = jax.random.uniform(jax.random.fold_in(jax.random.fold_in(key, 6), position), (shards_of,), jnp.float32, low / len(shards), largest / len(shards))
        gain = gain * jnp.repeat(jnp.exp(steps), shape[position] // shards_of).reshape((-1,) + (1,) * (len(shape) - 1 - position))
    return gain


def deal_out(key, own, number, rows, count, top, most, skew):
    ranking = jax.random.permutation(key, count)
    packed, common = portions_of(count, rows * top, most, skew, True), portions_of(count, rows * top, most, skew, False)
    places = jnp.arange(count)

    def named(sizes, rotation):
        used = int((sizes > 0).sum())
        fixed = max(1, used // 4)
        shifted = fixed + (places - fixed + rotation * (used - fixed)) % max(1, count - fixed)
        return jnp.zeros((count,), jnp.int32).at[ranking[jnp.where(places < fixed, places, shifted)]].set(jnp.asarray(sizes, jnp.int32))

    sizes = jnp.where(number % 4 == 0, named(packed, number // 4), named(common, number - number // 4 - 1))
    mixed = jax.random.permutation(jax.random.fold_in(own, 3), count)
    source_of, taker = mixed[0:count // 2 * 2:2], mixed[1:count // 2 * 2:2]
    margin = jnp.minimum(sizes[source_of] - 1, most - sizes[taker]) // 2
    margin = jnp.where((source_of == ranking[0]) | (taker == ranking[0]) | (sizes[taker] == 0), 0, jnp.maximum(margin, 0))
    shifted = jax.random.randint(jax.random.fold_in(own, 4), (count // 2,), 0, 1 << 20) % (margin + 1)
    sizes = sizes.at[source_of].add(-shifted).at[taker].add(shifted)
    members = jnp.searchsorted(jnp.cumsum(sizes), jnp.arange(rows * top), side="right").astype(jnp.int32)
    listing = members.reshape(top, rows).T
    listing = listing[jax.random.permutation(jax.random.fold_in(own, 1), rows)]
    rotation = jax.random.randint(jax.random.fold_in(own, 2), (rows, 1), 0, top)
    return jnp.take_along_axis(listing, (jnp.arange(top)[None, :] + rotation) % top, axis=1)


def portions_of(amount, total, limit, lean, full):
    loads = [(1 << 20) // math.isqrt(rank ** lean) + 1 for rank in range(1, amount + 1)]
    largest = limit if full else min(limit, max(-(-total // amount), total * loads[0] // sum(loads)))
    least = 1 if total - largest >= amount - 1 else 0
    counts, spare = [largest] + [least] * (amount - 1), total - largest - least * (amount - 1)
    while spare > 0:
        free = [i for i in range(1, amount) if counts[i] < largest] or [i for i in range(1, amount) if counts[i] < limit]
        mass, budget = sum([loads[i] for i in free]), spare
        for i in free:
            addition = min(limit - counts[i], max(1, budget * loads[i] // mass), spare)
            counts[i] = counts[i] + addition
            spare = spare - addition
    return np.array(counts)


def centred(stream_key, dims, scale, bound, cuts=(), kind=jnp.bfloat16):
    loudness = block_levels(stream_key, dims, cuts, -0.22, 0.18) if cuts else 1.0
    drawn = jax.random.normal(stream_key, dims, jnp.float32) * scale * loudness
    return jnp.minimum(jnp.maximum(drawn, -bound), bound).astype(kind)


def setup_inputs(seed: int = 0) -> dict:
    splits = jax.random.split(jax.random.key(seed), 9)
    ground_accel = centred(splits[0], (RECORDS, SPAN), 1.0, 6.0)
    modal_kernel = centred(splits[1], (MODES, TAPS), TAPS ** -0.5, 0.25, ((0, 32),))
    mode_shapes = centred(splits[2], (MEMBERS * COMPS, MODES), MODES ** -0.5, 0.09375, ((0, 8), (1, 4)))
    member_owner_keys = jax.random.split(jax.random.fold_in(splits[3], 1), MEMBERS // (MEM_DEV // N_MODE))
    member_owner_turns = jax.random.permutation(jax.random.fold_in(splits[3], 3), MEMBERS // (MEM_DEV // N_MODE))
    member_owner = jax.vmap(lambda own, number: deal_out(jax.random.fold_in(splits[3], 2), own, number, MEM_DEV // N_MODE, N_MODE * N_MEMBER, 1, CAP, 2))(member_owner_keys, member_owner_turns).reshape((MEMBERS, 1))
    member_group = plant(jax.random.randint(splits[4], (MEMBERS, 1), 0, GROUP_DEV), jax.random.fold_in(splits[4], 1), 0, GROUP_DEV - 1).astype(jnp.int32)
    record_table = plant(jax.random.randint(splits[5], (GROUPS, CASES), 0, RECORDS), jax.random.fold_in(splits[5], 1), 0, RECORDS - 1).astype(jnp.int32)
    case_coef = centred(splits[6], (CASES, COMPS), 0.3, 1.5, (), jnp.float32)
    gravity = centred(splits[7], (GROUPS, CASES), 2.0, 10.0, ((0, 32),), jnp.float32)
    return {"ground_accel": ground_accel, "modal_kernel": modal_kernel, "mode_shapes": mode_shapes, "member_owner": member_owner, "member_group": member_group, "record_table": record_table, "case_coef": case_coef, "gravity": gravity}


def reference(ground_accel, modal_kernel, mode_shapes, member_owner, member_group, record_table, case_coef, gravity):
    offsets = TAPS - 1 + jnp.arange(TW)[None, :] - jnp.arange(TAPS)[:, None]
    lagged = jnp.transpose(ground_accel[:, offsets], (1, 0, 2)).reshape(TAPS, RECORDS * TW)
    modal_resp = jnp.dot(modal_kernel, lagged, preferred_element_type=jnp.float32).astype(jnp.bfloat16)
    block_modes = MODES // N_MODE

    def add_block(running, block_index):
        first_mode = (block_index * block_modes).astype(jnp.int32)
        shapes = lax.dynamic_slice_in_dim(mode_shapes, first_mode, block_modes, 1)
        resp_rows = lax.dynamic_slice_in_dim(modal_resp, first_mode, block_modes, 0)
        partial_term = jnp.dot(shapes, resp_rows, preferred_element_type=jnp.float32).astype(jnp.bfloat16)
        partial_term = lax.optimization_barrier(partial_term)
        return running + partial_term.astype(jnp.float32), None

    start_total = jnp.zeros((MEMBERS * COMPS, RECORDS * TW), jnp.float32)
    forces = lax.scan(add_block, start_total, jnp.arange(N_MODE, dtype=jnp.int32))[0]
    group_index = (member_owner[:, 0] * GROUP_DEV + member_group[:, 0]).astype(jnp.int32)
    group_sums = jax.ops.segment_sum(forces.reshape(MEMBERS, COMPS * RECORDS * TW), group_index, num_segments=GROUPS)
    group_sums = group_sums.reshape(GROUPS, COMPS, RECORDS, TW)
    case_mix = jnp.einsum("sc,gcrt->gsrt", case_coef.astype(jnp.float32), group_sums, precision=lax.Precision.HIGHEST)
    record_pick = (record_table[:, :, None] == jnp.arange(RECORDS, dtype=jnp.int32)[None, None, :]).astype(jnp.float32)
    selected = jnp.sum(record_pick[:, :, :, None] * case_mix, axis=2)
    combined = gravity[:, :, None] + selected
    return jnp.max(jnp.abs(combined), axis=2)
```

```python
import functools

import jax
import jax.numpy as jnp
from jax import lax
from jax.experimental import pallas as pl
from jax.experimental.pallas import tpu as pltpu
from jax.sharding import PartitionSpec as P

MESH = pl.DeviceIdType.MESH
BF = jnp.bfloat16
F32 = jnp.float32


def kernel(
    dims,
    accel_ref,
    kern_ref,
    shapes_ref,
    code_ref,
    rec_ref,
    mix_ref,
    grav_ref,
    out_ref,
    mbuf,
    kbuf,
    recbuf,
    acc,
    lagged,
    sums,
    xbuf,
    abuf,
    ybuf,
    bbuf,
    msem,
    loc_sem,
    z_send,
    z_recv,
    y_send,
    y_recv,
    zr_send,
    zr_recv,
    yr_send,
    yr_recv,
    mr_send,
    mr_recv,
    a_send,
    a_recv,
    b_send,
    b_recv,
):
    n_mode, n_member, nz, ny, comps, own_rows = dims
    n_records = accel_ref.shape[0]
    taps = kern_ref.shape[1]
    shard = kern_ref.shape[0]
    n_chunk, chunk = code_ref.shape
    group_rows = acc.shape[0]
    mode = lax.axis_index("mode")
    member = lax.axis_index("member")
    z = member // ny
    y = lax.rem(member, ny)
    slab = n_member * own_rows

    def load(i):
        rows = pl.ds(pl.multiple_of(i * chunk, chunk), chunk)
        return pltpu.make_async_copy(shapes_ref.at[rows, :], mbuf.at[rows, :], msem.at[i])

    for i in range(n_chunk):
        load(i).start()

    def member_at(zz, yy):
        return zz * ny + yy

    def krows(m):
        return pl.ds(pl.multiple_of(m * shard, shard), shard)

    def rrows(b, m):
        return pl.ds(pl.multiple_of((b * n_member + m) * own_rows, own_rows), own_rows)

    own_k = pltpu.make_async_copy(kern_ref, kbuf.at[krows(member), :], loc_sem.at[0])
    own_k.start()
    own_r = pltpu.make_async_copy(rec_ref, recbuf.at[rrows(mode, member), :], loc_sem.at[1])
    own_r.start()

    barrier = pltpu.get_barrier_semaphore()
    for d in range(1, n_member):
        pl.semaphore_signal(
            barrier, inc=1, device_id={"member": lax.rem(member + d, n_member)}, device_id_type=MESH
        )
    for d in range(1, n_mode):
        pl.semaphore_signal(
            barrier, inc=1, device_id={"mode": lax.rem(mode + d, n_mode)}, device_id_type=MESH
        )
    pl.semaphore_wait(barrier, n_member + n_mode - 2)

    def remote(src, dst, send, recv, target):
        return pltpu.make_async_remote_copy(
            src_ref=src,
            dst_ref=dst,
            send_sem=send,
            recv_sem=recv,
            device_id=target,
            device_id_type=MESH,
        )

    sent = []
    z_copies, zr_copies, y_copies, yr_copies = {}, {}, {}, {}

    def send_y(d):
        source = member_at(lax.rem(z + nz - d, nz), y)
        for e in range(1, ny):
            target = {"member": member_at(z, lax.rem(y + e, ny))}
            kr, rr = krows(source), rrows(mode, source)
            ksrc = kern_ref if d == 0 else kbuf.at[kr, :]
            rsrc = rec_ref if d == 0 else recbuf.at[rr, :]
            y_copies[d, e] = remote(
                ksrc, kbuf.at[kr, :], y_send.at[d, e - 1], y_recv.at[d, e - 1], target
            )
            yr_copies[d, e] = remote(
                rsrc, recbuf.at[rr, :], yr_send.at[d, e - 1], yr_recv.at[d, e - 1], target
            )
            yr_copies[d, e].start()
            y_copies[d, e].start()

    for d in range(1, nz):
        target = {"member": member_at(lax.rem(z + d, nz), y)}
        z_copies[d] = remote(
            kern_ref, kbuf.at[krows(member), :], z_send.at[d - 1], z_recv.at[d - 1], target
        )
        zr_copies[d] = remote(
            rec_ref,
            recbuf.at[rrows(mode, member), :],
            zr_send.at[d - 1],
            zr_recv.at[d - 1],
            target,
        )
        zr_copies[d].start()
    send_y(0)
    for d in range(1, nz):
        z_copies[d].start()

    steps = lagged.shape[1] // n_records
    for r in range(n_records):
        for q in range(taps // steps):
            start = taps - steps * (q + 1)
            piece = jnp.broadcast_to(accel_ref[r : r + 1, start : start + 2 * steps], (steps, 2 * steps))
            rolled = pltpu.roll(piece, steps + 1, 1, stride=1, stride_axis=0)
            lagged[q * steps : (q + 1) * steps, r * steps : (r + 1) * steps] = rolled[
                :, :steps
            ].astype(BF)

    acc[...] = jnp.zeros_like(acc)
    part = chunk if group_rows % chunk == 0 else group_rows

    def chunk_step(i, carry):
        load(i).wait()
        code = code_ref[pl.ds(i, 1), :]
        block = mbuf[pl.ds(pl.multiple_of(i * chunk, chunk), chunk), :]

        def row_step(p, inner):
            first = pl.multiple_of(p * part, part)
            rows = lax.broadcasted_iota(jnp.int32, (part, chunk), 0) + first
            hot = jnp.where(rows == code, 1.0, 0.0).astype(BF)
            acc[pl.ds(first, part), :] += jnp.dot(hot, block, preferred_element_type=F32)
            return inner

        return lax.fori_loop(0, group_rows // part, row_step, carry)

    marks = [(n_chunk * (d + 1)) // (nz + 1) for d in range(1, nz)]
    done = 0
    for d in range(1, nz):
        lax.fori_loop(done, marks[d - 1], chunk_step, 0)
        done = marks[d - 1]
        z_copies[d].wait_recv()
        zr_copies[d].wait_recv()
        send_y(d)
    lax.fori_loop(done, n_chunk, chunk_step, 0)

    own_k.wait()
    own_r.wait()
    for d in range(nz):
        for e in range(1, ny):
            yr_copies[d, e].wait_recv()
    mine = pl.ds(pl.multiple_of(mode * slab, slab), slab)
    mr_copies = []
    for d in range(1, n_mode):
        copy = remote(
            recbuf.at[mine, :],
            recbuf.at[mine, :],
            mr_send.at[d - 1],
            mr_recv.at[d - 1],
            {"mode": lax.rem(mode + d, n_mode)},
        )
        copy.start()
        mr_copies.append(copy)
    for d in range(nz):
        for e in range(1, ny):
            y_copies[d, e].wait_recv()

    def contract(p, carry):
        rows = pl.ds(pl.multiple_of(p * part, part), part)
        by_tap = jnp.dot(acc[rows, :].astype(BF), kbuf[...], preferred_element_type=F32)
        sums[rows, :] = jnp.dot(
            by_tap.astype(BF), lagged[...], preferred_element_type=F32
        ).astype(BF)
        return carry

    lax.fori_loop(0, group_rows // part, contract, 0)
    for copy in mr_copies:
        copy.wait_recv()

    mixed_rows, mixed_from = mix_ref.shape[1:]

    def mix_slab(target):
        for k in range(slab // mixed_rows):
            to = pl.ds(
                pl.multiple_of(target * slab + k * mixed_rows, mixed_rows), mixed_rows
            )
            start = (target * (slab // mixed_rows) + k) * mixed_from
            got = sums[pl.ds(pl.multiple_of(start, mixed_from), mixed_from), :]
            mixed = jnp.dot(mix_ref[0], got, preferred_element_type=F32) + jnp.dot(
                mix_ref[1], got, preferred_element_type=F32
            )
            wanted = recbuf[to, :].astype(F32)
            picked = jnp.zeros((mixed_rows, steps), F32)
            for r in range(n_records):
                picked = jnp.where(wanted == r, mixed[:, r * steps : (r + 1) * steps], picked)
            xbuf[to, :] = picked.astype(BF)

    a_copies = []
    for d in range(n_mode - 1, 0, -1):
        target = lax.rem(mode + d, n_mode)
        mix_slab(target)
        copy = remote(
            xbuf.at[pl.ds(pl.multiple_of(target * slab, slab), slab), :],
            abuf.at[d - 1],
            a_send.at[d - 1],
            a_recv.at[d - 1],
            {"mode": target},
        )
        copy.start()
        a_copies.append((d, copy))
    mix_slab(mode)
    total = xbuf[mine, :].astype(F32)
    for d, copy in a_copies:
        copy.wait_recv()
        total = total + abuf[d - 1].astype(F32)
    ybuf[...] = total.astype(BF)

    b_copies = []
    for d in range(1, n_member):
        target = lax.rem(member + d, n_member)
        copy = remote(
            ybuf.at[pl.ds(pl.multiple_of(target * own_rows, own_rows), own_rows), :],
            bbuf.at[d - 1],
            b_send.at[d - 1],
            b_recv.at[d - 1],
            {"member": target},
        )
        copy.start()
        b_copies.append(copy)
    own = ybuf[pl.ds(pl.multiple_of(member * own_rows, own_rows), own_rows), :].astype(F32)
    for d, copy in enumerate(b_copies):
        copy.wait_recv()
        own = own + bbuf[d].astype(F32)
    out_ref[...] = jnp.max(jnp.abs(own + grav_ref[...]), axis=1, keepdims=True)

    for copies in (z_copies, zr_copies, y_copies, yr_copies):
        for copy in copies.values():
            copy.wait_send()
    for copy in mr_copies + b_copies + [c for _, c in a_copies]:
        copy.wait_send()


def local(
    n_mode,
    n_member,
    ground_accel,
    modal_kernel,
    mode_shapes,
    member_owner,
    member_group,
    record_table,
    case_coef,
    gravity,
):
    nz = 4
    ny = n_member // nz
    n_records, span = ground_accel.shape
    shard, taps = modal_kernel.shape
    steps = span - taps + 1
    cases, comps = case_coef.shape
    own_groups = gravity.shape[0]
    own_rows = own_groups * cases
    groups = n_mode * n_member * own_groups
    rows, modes = mode_shapes.shape
    chunk = 128 * comps
    n_chunk = rows // chunk
    group_rows = groups * comps

    accel = jnp.pad(ground_accel.astype(F32), ((0, 0), (0, taps + steps - span)))
    group = (member_owner * own_groups + member_group) * comps
    code = (group + jnp.arange(comps)[None, :]).reshape(n_chunk, chunk)
    rec = jnp.broadcast_to(record_table.astype(BF).reshape(own_rows, 1), (own_rows, steps))
    mix_groups = 32
    mix = jnp.kron(jnp.eye(mix_groups, dtype=F32), case_coef)
    high = mix.astype(BF)
    mix = jnp.stack([high, (mix - high.astype(F32)).astype(BF)])
    grav = gravity.reshape(own_rows, 1)

    vmem = pl.BlockSpec(memory_space=pltpu.VMEM)
    anywhere = pl.BlockSpec(memory_space=pl.ANY)
    dma = pltpu.SemaphoreType.DMA
    slab = n_member * own_rows
    out = pl.pallas_call(
        functools.partial(kernel, (n_mode, n_member, nz, ny, comps, own_rows)),
        out_shape=jax.ShapeDtypeStruct((own_rows, 1), F32),
        in_specs=[vmem, anywhere, anywhere, vmem, vmem, vmem, vmem],
        out_specs=vmem,
        scratch_shapes=[
            pltpu.VMEM((rows, modes), BF),
            pltpu.VMEM((n_member * shard, taps), BF),
            pltpu.VMEM((groups * cases, steps), BF),
            pltpu.VMEM((group_rows, modes), F32),
            pltpu.VMEM((taps, n_records * steps), BF),
            pltpu.VMEM((group_rows, n_records * steps), BF),
            pltpu.VMEM((groups * cases, steps), BF),
            pltpu.VMEM((n_mode - 1, slab, steps), BF),
            pltpu.VMEM((slab, steps), BF),
            pltpu.VMEM((n_member - 1, own_rows, steps), BF),
            dma((n_chunk,)),
            dma((2,)),
            dma((nz - 1,)),
            dma((nz - 1,)),
            dma((nz, ny - 1)),
            dma((nz, ny - 1)),
            dma((nz - 1,)),
            dma((nz - 1,)),
            dma((nz, ny - 1)),
            dma((nz, ny - 1)),
            dma((n_mode - 1,)),
            dma((n_mode - 1,)),
            dma((n_mode - 1,)),
            dma((n_mode - 1,)),
            dma((n_member - 1,)),
            dma((n_member - 1,)),
        ],
        compiler_params=pltpu.CompilerParams(
            collective_id=0, has_side_effects=True, vmem_limit_bytes=60 * 1024 * 1024
        ),
        cost_estimate=pl.CostEstimate(
            flops=2 * group_rows * rows * modes, bytes_accessed=2 * rows * modes, transcendentals=0
        ),
    )(accel, modal_kernel, mode_shapes, code, rec, mix, grav)
    return out.reshape(own_groups, cases)


def solution(mesh):
    placed = (
        P(),
        P(("mode", "member"), None),
        P("member", "mode"),
        P("member", None),
        P("member", None),
        P(("mode", "member"), None),
        P(),
        P(("mode", "member"), None),
    )
    return jax.shard_map(
        functools.partial(local, mesh.shape["mode"], mesh.shape["member"]),
        mesh=mesh,
        in_specs=placed,
        out_specs=P(("mode", "member"), None),
        check_vma=False,
    )
```

```python
import functools

import jax
import jax.numpy as jnp
from jax import lax
from jax.experimental import pallas as pl
from jax.experimental.pallas import tpu as pltpu
from jax.sharding import PartitionSpec as P

MESH = pl.DeviceIdType.MESH
BF = jnp.bfloat16
F32 = jnp.float32


def kernel(
    dims,
    accel_ref,
    kern_ref,
    shapes_ref,
    owner_ref,
    group_ref,
    table_ref,
    coef_ref,
    grav_ref,
    out_ref,
    mbuf,
    kbuf,
    recbuf,
    acc,
    lagged,
    sums,
    xbuf,
    abuf,
    ybuf,
    bbuf,
    mix_ref,
    padded,
    code_ref,
    rec_ref,
    msem,
    loc_sem,
    z_send,
    z_recv,
    y_send,
    y_recv,
    zr_send,
    zr_recv,
    yr_send,
    yr_recv,
    mr_send,
    mr_recv,
    a_send,
    a_recv,
    b_send,
    b_recv,
):
    n_mode, n_member, nz, ny, comps, own_rows = dims
    n_records = accel_ref.shape[0]
    taps = kern_ref.shape[1]
    shard = kern_ref.shape[0]
    n_chunk, chunk = code_ref.shape
    group_rows = acc.shape[0]
    mode = lax.axis_index("mode")
    member = lax.axis_index("member")
    z = member // ny
    y = lax.rem(member, ny)
    slab = n_member * own_rows

    def load(i):
        rows = pl.ds(pl.multiple_of(i * chunk, chunk), chunk)
        return pltpu.make_async_copy(shapes_ref.at[rows, :], mbuf.at[rows, :], msem.at[i])

    for i in range(n_chunk):
        load(i).start()

    table = table_ref[...].astype(F32)
    rec_ref[...] = (
        jnp.broadcast_to(table[:, :, None], table.shape + (rec_ref.shape[1],))
        .reshape(rec_ref.shape)
        .astype(BF)
    )

    def member_at(zz, yy):
        return zz * ny + yy

    def krows(m):
        return pl.ds(pl.multiple_of(m * shard, shard), shard)

    def rrows(b, m):
        return pl.ds(pl.multiple_of((b * n_member + m) * own_rows, own_rows), own_rows)

    own_k = pltpu.make_async_copy(kern_ref, kbuf.at[krows(member), :], loc_sem.at[0])
    own_k.start()
    own_r = pltpu.make_async_copy(rec_ref, recbuf.at[rrows(mode, member), :], loc_sem.at[1])
    own_r.start()

    barrier = pltpu.get_barrier_semaphore()
    for d in range(1, n_member):
        pl.semaphore_signal(
            barrier, inc=1, device_id={"member": lax.rem(member + d, n_member)}, device_id_type=MESH
        )
    for d in range(1, n_mode):
        pl.semaphore_signal(
            barrier, inc=1, device_id={"mode": lax.rem(mode + d, n_mode)}, device_id_type=MESH
        )
    pl.semaphore_wait(barrier, n_member + n_mode - 2)

    def remote(src, dst, send, recv, target):
        return pltpu.make_async_remote_copy(
            src_ref=src,
            dst_ref=dst,
            send_sem=send,
            recv_sem=recv,
            device_id=target,
            device_id_type=MESH,
        )

    sent = []
    z_copies, zr_copies, y_copies, yr_copies = {}, {}, {}, {}

    def send_y(d):
        source = member_at(lax.rem(z + nz - d, nz), y)
        for e in range(1, ny):
            target = {"member": member_at(z, lax.rem(y + e, ny))}
            kr, rr = krows(source), rrows(mode, source)
            ksrc = kern_ref if d == 0 else kbuf.at[kr, :]
            rsrc = rec_ref if d == 0 else recbuf.at[rr, :]
            y_copies[d, e] = remote(
                ksrc, kbuf.at[kr, :], y_send.at[d, e - 1], y_recv.at[d, e - 1], target
            )
            yr_copies[d, e] = remote(
                rsrc, recbuf.at[rr, :], yr_send.at[d, e - 1], yr_recv.at[d, e - 1], target
            )
            yr_copies[d, e].start()
            y_copies[d, e].start()

    for d in range(1, nz):
        target = {"member": member_at(lax.rem(z + d, nz), y)}
        z_copies[d] = remote(
            kern_ref, kbuf.at[krows(member), :], z_send.at[d - 1], z_recv.at[d - 1], target
        )
        zr_copies[d] = remote(
            rec_ref,
            recbuf.at[rrows(mode, member), :],
            zr_send.at[d - 1],
            zr_recv.at[d - 1],
            target,
        )
        zr_copies[d].start()
    send_y(0)
    for d in range(1, nz):
        z_copies[d].start()

    steps = lagged.shape[1] // n_records
    span = accel_ref.shape[1]
    padded[...] = jnp.zeros_like(padded)
    padded[:, :span] = accel_ref[...].astype(F32)
    for r in range(n_records):
        for q in range(taps // steps):
            start = taps - steps * (q + 1)
            piece = jnp.broadcast_to(padded[r : r + 1, start : start + 2 * steps], (steps, 2 * steps))
            rolled = pltpu.roll(piece, steps + 1, 1, stride=1, stride_axis=0)
            lagged[q * steps : (q + 1) * steps, r * steps : (r + 1) * steps] = rolled[
                :, :steps
            ].astype(BF)

    cases = coef_ref.shape[0]
    mixed_rows, mixed_from = mix_ref.shape[1:]
    stacked = jnp.concatenate([coef_ref[...]] * (mixed_rows // cases), axis=0)
    at_row = lax.broadcasted_iota(jnp.int32, (mixed_rows, mixed_from), 0) // cases
    offset = lax.broadcasted_iota(jnp.int32, (mixed_rows, mixed_from), 1) - comps * at_row
    mix = jnp.zeros((mixed_rows, mixed_from), F32)
    for c in range(comps):
        mix = jnp.where(offset == c, stacked[:, c : c + 1], mix)
    mix_ref[0] = mix.astype(BF)
    mix_ref[1] = (mix - mix.astype(BF).astype(F32)).astype(BF)

    wide = (chunk // comps, chunk)
    place = lax.broadcasted_iota(jnp.int32, wide, 1) - comps * lax.broadcasted_iota(
        jnp.int32, wide, 0
    )
    inside = (place >= 0) & (place < comps)
    spread = jnp.where(inside, 1.0, 0.0).astype(BF)
    comp = jnp.sum(jnp.where(inside, place, 0), axis=0, keepdims=True).astype(F32)
    owners = jnp.dot(owner_ref[...].astype(F32).astype(BF), spread, preferred_element_type=F32)
    groups = jnp.dot(group_ref[...].astype(F32).astype(BF), spread, preferred_element_type=F32)
    own_groups = table_ref.shape[0]
    code_ref[...] = ((owners * own_groups + groups) * comps + comp).astype(jnp.int32)

    acc[...] = jnp.zeros_like(acc)
    part = chunk if group_rows % chunk == 0 else group_rows

    def chunk_step(i, carry):
        load(i).wait()
        code = code_ref[pl.ds(i, 1), :]
        block = mbuf[pl.ds(pl.multiple_of(i * chunk, chunk), chunk), :]

        def row_step(p, inner):
            first = pl.multiple_of(p * part, part)
            rows = lax.broadcasted_iota(jnp.int32, (part, chunk), 0) + first
            hot = jnp.where(rows == code, 1.0, 0.0).astype(BF)
            acc[pl.ds(first, part), :] += jnp.dot(hot, block, preferred_element_type=F32)
            return inner

        return lax.fori_loop(0, group_rows // part, row_step, carry)

    marks = [(n_chunk * (d + 1)) // (nz + 1) for d in range(1, nz)]
    done = 0
    for d in range(1, nz):
        lax.fori_loop(done, marks[d - 1], chunk_step, 0)
        done = marks[d - 1]
        z_copies[d].wait_recv()
        zr_copies[d].wait_recv()
        send_y(d)
    lax.fori_loop(done, n_chunk, chunk_step, 0)

    own_k.wait()
    own_r.wait()
    for d in range(nz):
        for e in range(1, ny):
            yr_copies[d, e].wait_recv()
    mine = pl.ds(pl.multiple_of(mode * slab, slab), slab)
    mr_copies = []
    for d in range(1, n_mode):
        copy = remote(
            recbuf.at[mine, :],
            recbuf.at[mine, :],
            mr_send.at[d - 1],
            mr_recv.at[d - 1],
            {"mode": lax.rem(mode + d, n_mode)},
        )
        copy.start()
        mr_copies.append(copy)
    for d in range(nz):
        for e in range(1, ny):
            y_copies[d, e].wait_recv()

    def contract(p, carry):
        rows = pl.ds(pl.multiple_of(p * part, part), part)
        by_tap = jnp.dot(acc[rows, :].astype(BF), kbuf[...], preferred_element_type=F32)
        sums[rows, :] = jnp.dot(
            by_tap.astype(BF), lagged[...], preferred_element_type=F32
        ).astype(BF)
        return carry

    lax.fori_loop(0, group_rows // part, contract, 0)
    for copy in mr_copies:
        copy.wait_recv()

    def mix_slab(target):
        for k in range(slab // mixed_rows):
            to = pl.ds(
                pl.multiple_of(target * slab + k * mixed_rows, mixed_rows), mixed_rows
            )
            start = (target * (slab // mixed_rows) + k) * mixed_from
            got = sums[pl.ds(pl.multiple_of(start, mixed_from), mixed_from), :]
            mixed = jnp.dot(mix_ref[0], got, preferred_element_type=F32) + jnp.dot(
                mix_ref[1], got, preferred_element_type=F32
            )
            wanted = recbuf[to, :].astype(F32)
            picked = jnp.zeros((mixed_rows, steps), F32)
            for r in range(n_records):
                picked = jnp.where(wanted == r, mixed[:, r * steps : (r + 1) * steps], picked)
            xbuf[to, :] = picked.astype(BF)

    a_copies = []
    for d in range(n_mode - 1, 0, -1):
        target = lax.rem(mode + d, n_mode)
        mix_slab(target)
        copy = remote(
            xbuf.at[pl.ds(pl.multiple_of(target * slab, slab), slab), :],
            abuf.at[d - 1],
            a_send.at[d - 1],
            a_recv.at[d - 1],
            {"mode": target},
        )
        copy.start()
        a_copies.append((d, copy))
    mix_slab(mode)
    total = xbuf[mine, :].astype(F32)
    for d, copy in a_copies:
        copy.wait_recv()
        total = total + abuf[d - 1].astype(F32)
    ybuf[...] = total.astype(BF)

    b_copies = []
    for d in range(1, n_member):
        target = lax.rem(member + d, n_member)
        copy = remote(
            ybuf.at[pl.ds(pl.multiple_of(target * own_rows, own_rows), own_rows), :],
            bbuf.at[d - 1],
            b_send.at[d - 1],
            b_recv.at[d - 1],
            {"member": target},
        )
        copy.start()
        b_copies.append(copy)
    own = ybuf[pl.ds(pl.multiple_of(member * own_rows, own_rows), own_rows), :].astype(F32)
    for d, copy in enumerate(b_copies):
        copy.wait_recv()
        own = own + bbuf[d].astype(F32)
    own = own.reshape(own_rows // cases, cases, steps)
    top = grav_ref[...] + jnp.max(own, axis=2)
    bottom = grav_ref[...] + jnp.min(own, axis=2)
    out_ref[...] = jnp.maximum(top, -bottom)

    for copies in (z_copies, zr_copies, y_copies, yr_copies):
        for copy in copies.values():
            copy.wait_send()
    for copy in mr_copies + b_copies + [c for _, c in a_copies]:
        copy.wait_send()


def local(
    n_mode,
    n_member,
    ground_accel,
    modal_kernel,
    mode_shapes,
    member_owner,
    member_group,
    record_table,
    case_coef,
    gravity,
):
    nz = 4
    ny = n_member // nz
    n_records, span = ground_accel.shape
    shard, taps = modal_kernel.shape
    steps = span - taps + 1
    cases, comps = case_coef.shape
    own_groups = gravity.shape[0]
    own_rows = own_groups * cases
    groups = n_mode * n_member * own_groups
    rows, modes = mode_shapes.shape
    chunk = 128 * comps
    n_chunk = rows // chunk
    group_rows = groups * comps

    by_chunk = (n_chunk, chunk // comps)
    mix_groups = 32

    vmem = pl.BlockSpec(memory_space=pltpu.VMEM)
    anywhere = pl.BlockSpec(memory_space=pl.ANY)
    dma = pltpu.SemaphoreType.DMA
    slab = n_member * own_rows
    out = pl.pallas_call(
        functools.partial(kernel, (n_mode, n_member, nz, ny, comps, own_rows)),
        out_shape=jax.ShapeDtypeStruct((own_groups, cases), F32),
        in_specs=[vmem, anywhere, anywhere, vmem, vmem, vmem, vmem, vmem],
        out_specs=vmem,
        scratch_shapes=[
            pltpu.VMEM((rows, modes), BF),
            pltpu.VMEM((n_member * shard, taps), BF),
            pltpu.VMEM((groups * cases, steps), BF),
            pltpu.VMEM((group_rows, modes), F32),
            pltpu.VMEM((taps, n_records * steps), BF),
            pltpu.VMEM((group_rows, n_records * steps), BF),
            pltpu.VMEM((groups * cases, steps), BF),
            pltpu.VMEM((n_mode - 1, slab, steps), BF),
            pltpu.VMEM((slab, steps), BF),
            pltpu.VMEM((n_member - 1, own_rows, steps), BF),
            pltpu.VMEM((2, mix_groups * cases, mix_groups * comps), BF),
            pltpu.VMEM((n_records, taps + steps), F32),
            pltpu.VMEM((n_chunk, chunk), jnp.int32),
            pltpu.VMEM((own_rows, steps), BF),
            dma((n_chunk,)),
            dma((2,)),
            dma((nz - 1,)),
            dma((nz - 1,)),
            dma((nz, ny - 1)),
            dma((nz, ny - 1)),
            dma((nz - 1,)),
            dma((nz - 1,)),
            dma((nz, ny - 1)),
            dma((nz, ny - 1)),
            dma((n_mode - 1,)),
            dma((n_mode - 1,)),
            dma((n_mode - 1,)),
            dma((n_mode - 1,)),
            dma((n_member - 1,)),
            dma((n_member - 1,)),
        ],
        compiler_params=pltpu.CompilerParams(
            collective_id=0, has_side_effects=True, vmem_limit_bytes=60 * 1024 * 1024
        ),
        cost_estimate=pl.CostEstimate(
            flops=2 * group_rows * rows * modes, bytes_accessed=2 * rows * modes, transcendentals=0
        ),
    )(
        ground_accel,
        modal_kernel,
        mode_shapes,
        member_owner.reshape(by_chunk),
        member_group.reshape(by_chunk),
        record_table,
        case_coef,
        gravity,
    )
    return out


def solution(mesh):
    placed = (
        P(),
        P(("mode", "member"), None),
        P("member", "mode"),
        P("member", None),
        P("member", None),
        P(("mode", "member"), None),
        P(),
        P(("mode", "member"), None),
    )
    return jax.shard_map(
        functools.partial(local, mesh.shape["mode"], mesh.shape["member"]),
        mesh=mesh,
        in_specs=placed,
        out_specs=P(("mode", "member"), None),
        check_vma=False,
    )
```

```python
import functools

import jax
import jax.numpy as jnp
from jax import lax
from jax.experimental import pallas as pl
from jax.experimental.pallas import tpu as pltpu
from jax.sharding import PartitionSpec as P

MESH = pl.DeviceIdType.MESH
BF = jnp.bfloat16
F32 = jnp.float32


def kernel(
    dims,
    accel_ref,
    kern_ref,
    shapes_ref,
    owner_ref,
    group_ref,
    table_ref,
    coef_ref,
    grav_ref,
    out_ref,
    mbuf,
    kbuf,
    recbuf,
    acc,
    lagged,
    sums,
    xbuf,
    abuf,
    ybuf,
    bbuf,
    mix_ref,
    padded,
    code_ref,
    order_ref,
    perm,
    rec_ref,
    msem,
    loc_sem,
    z_send,
    z_recv,
    y_send,
    y_recv,
    zr_send,
    zr_recv,
    yr_send,
    yr_recv,
    mr_send,
    mr_recv,
    a_send,
    a_recv,
    b_send,
    b_recv,
):
    n_mode, n_member, nz, ny, comps, own_rows = dims
    n_records = accel_ref.shape[0]
    taps = kern_ref.shape[1]
    shard = kern_ref.shape[0]
    n_chunk, chunk_members = owner_ref.shape
    chunk = chunk_members * comps
    group_rows = acc.shape[0]
    mode = lax.axis_index("mode")
    member = lax.axis_index("member")
    z = member // ny
    y = lax.rem(member, ny)
    slab = n_member * own_rows

    def load(i):
        rows = pl.ds(pl.multiple_of(i * chunk, chunk), chunk)
        return pltpu.make_async_copy(shapes_ref.at[rows, :], mbuf.at[rows, :], msem.at[i])

    for i in range(n_chunk):
        load(i).start()

    table = table_ref[...].astype(F32)
    rec_ref[...] = (
        jnp.broadcast_to(table[:, :, None], table.shape + (rec_ref.shape[1],))
        .reshape(rec_ref.shape)
        .astype(BF)
    )

    def member_at(zz, yy):
        return zz * ny + yy

    def krows(m):
        return pl.ds(pl.multiple_of(m * shard, shard), shard)

    def rrows(b, m):
        return pl.ds(pl.multiple_of((b * n_member + m) * own_rows, own_rows), own_rows)

    own_k = pltpu.make_async_copy(kern_ref, kbuf.at[krows(member), :], loc_sem.at[0])
    own_k.start()
    own_r = pltpu.make_async_copy(rec_ref, recbuf.at[rrows(mode, member), :], loc_sem.at[1])
    own_r.start()

    barrier = pltpu.get_barrier_semaphore()
    for d in range(1, n_member):
        pl.semaphore_signal(
            barrier, inc=1, device_id={"member": lax.rem(member + d, n_member)}, device_id_type=MESH
        )
    for d in range(1, n_mode):
        pl.semaphore_signal(
            barrier, inc=1, device_id={"mode": lax.rem(mode + d, n_mode)}, device_id_type=MESH
        )
    pl.semaphore_wait(barrier, n_member + n_mode - 2)

    def remote(src, dst, send, recv, target):
        return pltpu.make_async_remote_copy(
            src_ref=src,
            dst_ref=dst,
            send_sem=send,
            recv_sem=recv,
            device_id=target,
            device_id_type=MESH,
        )

    sent = []
    z_copies, zr_copies, y_copies, yr_copies = {}, {}, {}, {}

    def send_y(d):
        source = member_at(lax.rem(z + nz - d, nz), y)
        for e in range(1, ny):
            target = {"member": member_at(z, lax.rem(y + e, ny))}
            kr, rr = krows(source), rrows(mode, source)
            ksrc = kern_ref if d == 0 else kbuf.at[kr, :]
            rsrc = rec_ref if d == 0 else recbuf.at[rr, :]
            y_copies[d, e] = remote(
                ksrc, kbuf.at[kr, :], y_send.at[d, e - 1], y_recv.at[d, e - 1], target
            )
            yr_copies[d, e] = remote(
                rsrc, recbuf.at[rr, :], yr_send.at[d, e - 1], yr_recv.at[d, e - 1], target
            )
            yr_copies[d, e].start()
            y_copies[d, e].start()

    for d in range(1, nz):
        target = {"member": member_at(lax.rem(z + d, nz), y)}
        z_copies[d] = remote(
            kern_ref, kbuf.at[krows(member), :], z_send.at[d - 1], z_recv.at[d - 1], target
        )
        zr_copies[d] = remote(
            rec_ref,
            recbuf.at[rrows(mode, member), :],
            zr_send.at[d - 1],
            zr_recv.at[d - 1],
            target,
        )
        zr_copies[d].start()
    send_y(0)
    for d in range(1, nz):
        z_copies[d].start()

    steps = lagged.shape[1] // n_records
    span = accel_ref.shape[1]
    padded[...] = jnp.zeros_like(padded)
    padded[:, :span] = accel_ref[...].astype(F32)
    for r in range(n_records):
        for q in range(taps // steps):
            start = taps - steps * (q + 1)
            piece = jnp.broadcast_to(padded[r : r + 1, start : start + 2 * steps], (steps, 2 * steps))
            rolled = pltpu.roll(piece, steps + 1, 1, stride=1, stride_axis=0)
            lagged[q * steps : (q + 1) * steps, r * steps : (r + 1) * steps] = rolled[
                :, :steps
            ].astype(BF)

    cases = coef_ref.shape[0]
    mixed_rows, mixed_from = mix_ref.shape[1:]
    stacked = jnp.concatenate([coef_ref[...]] * (mixed_rows // cases), axis=0)
    at_row = lax.broadcasted_iota(jnp.int32, (mixed_rows, mixed_from), 0) // cases
    mixed_groups = mixed_from // comps
    offset = lax.broadcasted_iota(jnp.int32, (mixed_rows, mixed_from), 1) - at_row
    mix = jnp.zeros((mixed_rows, mixed_from), F32)
    for c in range(comps):
        mix = jnp.where(offset == c * mixed_groups, stacked[:, c : c + 1], mix)
    mix_ref[0] = mix.astype(BF)
    mix_ref[1] = (mix - mix.astype(BF).astype(F32)).astype(BF)

    code_ref[...] = owner_ref[...] * table_ref.shape[0] + group_ref[...]
    few = order_ref.shape[0] // comps
    to_row = lax.broadcasted_iota(jnp.int32, order_ref.shape, 0)
    from_row = lax.broadcasted_iota(jnp.int32, order_ref.shape, 1)
    wanted_row = comps * (to_row - few * (to_row // few)) + to_row // few
    order_ref[...] = jnp.where(from_row == wanted_row, 1.0, 0.0).astype(BF)

    acc[...] = jnp.zeros_like(acc)
    part = 128 * comps
    groups = group_rows // comps

    def chunk_step(i, carry):
        load(i).wait()
        code = code_ref[pl.ds(i, 1), :]
        hot = jnp.where(
            lax.broadcasted_iota(jnp.int32, (groups, chunk_members), 0) == code, 1.0, 0.0
        ).astype(BF)
        size = few * comps
        for k in range(chunk // size):
            rows = pl.ds(pl.multiple_of(i * chunk + k * size, size), size)
            ordered = jnp.dot(order_ref[...], mbuf[rows, :], preferred_element_type=F32).astype(BF)
            for c in range(comps):
                perm[pl.ds(c * chunk_members + k * few, few), :] = ordered[
                    c * few : (c + 1) * few
                ]
        for c in range(comps):
            acc[pl.ds(c * groups, groups), :] += jnp.dot(
                hot,
                perm[pl.ds(c * chunk_members, chunk_members), :],
                preferred_element_type=F32,
            )
        return carry

    marks = [(n_chunk * d) // nz for d in range(1, nz)]
    done = 0
    for d in range(1, nz):
        lax.fori_loop(done, marks[d - 1], chunk_step, 0)
        done = marks[d - 1]
        z_copies[d].wait_recv()
        zr_copies[d].wait_recv()
        send_y(d)
    lax.fori_loop(done, n_chunk, chunk_step, 0)

    own_k.wait()
    own_r.wait()
    for d in range(nz):
        for e in range(1, ny):
            yr_copies[d, e].wait_recv()
    mine = pl.ds(pl.multiple_of(mode * slab, slab), slab)
    mr_copies = []
    for d in range(1, n_mode):
        copy = remote(
            recbuf.at[mine, :],
            recbuf.at[mine, :],
            mr_send.at[d - 1],
            mr_recv.at[d - 1],
            {"mode": lax.rem(mode + d, n_mode)},
        )
        copy.start()
        mr_copies.append(copy)
    for d in range(nz):
        for e in range(1, ny):
            y_copies[d, e].wait_recv()

    def contract(p, carry):
        rows = pl.ds(pl.multiple_of(p * part, part), part)
        by_tap = jnp.dot(acc[rows, :].astype(BF), kbuf[...], preferred_element_type=F32)
        sums[rows, :] = jnp.dot(
            by_tap.astype(BF), lagged[...], preferred_element_type=F32
        ).astype(BF)
        return carry

    lax.fori_loop(0, group_rows // part, contract, 0)
    for copy in mr_copies:
        copy.wait_recv()

    def mix_slab(target):
        for k in range(slab // mixed_rows):
            to = pl.ds(
                pl.multiple_of(target * slab + k * mixed_rows, mixed_rows), mixed_rows
            )
            start = (target * (slab // mixed_rows) + k) * mixed_groups
            got = jnp.concatenate(
                [
                    sums[
                        pl.ds(pl.multiple_of(start + c * groups, mixed_groups), mixed_groups), :
                    ]
                    for c in range(comps)
                ],
                axis=0,
            )
            mixed = jnp.dot(mix_ref[0], got, preferred_element_type=F32) + jnp.dot(
                mix_ref[1], got, preferred_element_type=F32
            )
            wanted = recbuf[to, :].astype(F32)
            picked = jnp.zeros((mixed_rows, steps), F32)
            for r in range(n_records):
                picked = jnp.where(wanted == r, mixed[:, r * steps : (r + 1) * steps], picked)
            xbuf[to, :] = picked.astype(BF)

    a_copies = []
    for d in range(n_mode - 1, 0, -1):
        target = lax.rem(mode + d, n_mode)
        mix_slab(target)
        copy = remote(
            xbuf.at[pl.ds(pl.multiple_of(target * slab, slab), slab), :],
            abuf.at[d - 1],
            a_send.at[d - 1],
            a_recv.at[d - 1],
            {"mode": target},
        )
        copy.start()
        a_copies.append((d, copy))
    mix_slab(mode)
    total = xbuf[mine, :].astype(F32)
    for d, copy in a_copies:
        copy.wait_recv()
        total = total + abuf[d - 1].astype(F32)
    ybuf[...] = total.astype(BF)

    b_copies = []
    for d in range(1, n_member):
        target = lax.rem(member + d, n_member)
        copy = remote(
            ybuf.at[pl.ds(pl.multiple_of(target * own_rows, own_rows), own_rows), :],
            bbuf.at[d - 1],
            b_send.at[d - 1],
            b_recv.at[d - 1],
            {"member": target},
        )
        copy.start()
        b_copies.append(copy)
    own = ybuf[pl.ds(pl.multiple_of(member * own_rows, own_rows), own_rows), :].astype(F32)
    for d, copy in enumerate(b_copies):
        copy.wait_recv()
        own = own + bbuf[d].astype(F32)
    own = own.reshape(own_rows // cases, cases, steps)
    top = grav_ref[...] + jnp.max(own, axis=2)
    bottom = grav_ref[...] + jnp.min(own, axis=2)
    out_ref[...] = jnp.maximum(top, -bottom)

    for copies in (z_copies, zr_copies, y_copies, yr_copies):
        for copy in copies.values():
            copy.wait_send()
    for copy in mr_copies + b_copies + [c for _, c in a_copies]:
        copy.wait_send()


def local(
    n_mode,
    n_member,
    ground_accel,
    modal_kernel,
    mode_shapes,
    member_owner,
    member_group,
    record_table,
    case_coef,
    gravity,
):
    nz = 4
    ny = n_member // nz
    n_records, span = ground_accel.shape
    shard, taps = modal_kernel.shape
    steps = span - taps + 1
    cases, comps = case_coef.shape
    own_groups = gravity.shape[0]
    own_rows = own_groups * cases
    groups = n_mode * n_member * own_groups
    rows, modes = mode_shapes.shape
    chunk = 256 * comps
    n_chunk = rows // chunk
    group_rows = groups * comps

    by_chunk = (n_chunk, chunk // comps)
    mix_groups = 32

    vmem = pl.BlockSpec(memory_space=pltpu.VMEM)
    anywhere = pl.BlockSpec(memory_space=pl.ANY)
    dma = pltpu.SemaphoreType.DMA
    slab = n_member * own_rows
    out = pl.pallas_call(
        functools.partial(kernel, (n_mode, n_member, nz, ny, comps, own_rows)),
        out_shape=jax.ShapeDtypeStruct((own_groups, cases), F32),
        in_specs=[vmem, anywhere, anywhere, vmem, vmem, vmem, vmem, vmem],
        out_specs=vmem,
        scratch_shapes=[
            pltpu.VMEM((rows, modes), BF),
            pltpu.VMEM((n_member * shard, taps), BF),
            pltpu.VMEM((groups * cases, steps), BF),
            pltpu.VMEM((group_rows, modes), F32),
            pltpu.VMEM((taps, n_records * steps), BF),
            pltpu.VMEM((group_rows, n_records * steps), BF),
            pltpu.VMEM((groups * cases, steps), BF),
            pltpu.VMEM((n_mode - 1, slab, steps), BF),
            pltpu.VMEM((slab, steps), BF),
            pltpu.VMEM((n_member - 1, own_rows, steps), BF),
            pltpu.VMEM((2, mix_groups * cases, mix_groups * comps), BF),
            pltpu.VMEM((n_records, taps + steps), F32),
            pltpu.VMEM((n_chunk, chunk // comps), jnp.int32),
            pltpu.VMEM((32 * comps, 32 * comps), BF),
            pltpu.VMEM((chunk, modes), BF),
            pltpu.VMEM((own_rows, steps), BF),
            dma((n_chunk,)),
            dma((2,)),
            dma((nz - 1,)),
            dma((nz - 1,)),
            dma((nz, ny - 1)),
            dma((nz, ny - 1)),
            dma((nz - 1,)),
            dma((nz - 1,)),
            dma((nz, ny - 1)),
            dma((nz, ny - 1)),
            dma((n_mode - 1,)),
            dma((n_mode - 1,)),
            dma((n_mode - 1,)),
            dma((n_mode - 1,)),
            dma((n_member - 1,)),
            dma((n_member - 1,)),
        ],
        compiler_params=pltpu.CompilerParams(
            collective_id=0, has_side_effects=True, vmem_limit_bytes=60 * 1024 * 1024
        ),
        cost_estimate=pl.CostEstimate(
            flops=2 * group_rows * rows * modes, bytes_accessed=2 * rows * modes, transcendentals=0
        ),
    )(
        ground_accel,
        modal_kernel,
        mode_shapes,
        member_owner.reshape(by_chunk),
        member_group.reshape(by_chunk),
        record_table,
        case_coef,
        gravity,
    )
    return out


def solution(mesh):
    placed = (
        P(),
        P(("mode", "member"), None),
        P("member", "mode"),
        P("member", None),
        P("member", None),
        P(("mode", "member"), None),
        P(),
        P(("mode", "member"), None),
    )
    return jax.shard_map(
        functools.partial(local, mesh.shape["mode"], mesh.shape["member"]),
        mesh=mesh,
        in_specs=placed,
        out_specs=P(("mode", "member"), None),
        check_vma=False,
    )
```
